32 devices in a mesh: section: 2 (over x), rows: 4 (over y, core), cols: 4 (over z).
Axes of the slice: x: 2, y: 2, z: 4, core: 2. Of those that a mesh axis runs over, the one named last changes fastest.
Arguments:
- features: bfloat16 [2, 96, 96, 728], P(None, ('rows', 'cols')), may hold values from -6 to 6
- upstream: bfloat16 [2, 96, 96, 256], P(None, 'rows', 'cols'), may hold values from -0.046875 to 0.046875
- depth_mid: float32 [9, 728], replicated, may hold values from -2 to 2
- point_mid: bfloat16 [728, 728], replicated, may hold values from -0.21875 to 0.21875
- projection: bfloat16 [728, 2048], replicated, may hold values from -0.21875 to 0.21875
- depth_first: float32 [9, 2048], replicated, may hold values from -2 to 2
- point_first: bfloat16 [2048, 256], replicated, may hold values from -0.125 to 0.125
- depth_later: float32 [2, 9, 256], replicated, may hold values from -2 to 2
- point_later: bfloat16 [2, 256, 256], replicated, may hold values from -0.375 to 0.375
- joining: bfloat16 [768, 256], replicated, may hold values from -0.21875 to 0.21875
- rate_first: int32 [2], replicated, may hold values from 1 to 6, as said below
- rates_later: int32 [2, 2], replicated, may hold values from 1 to 21, as said below
Outputs:
- grad_mid: float32 [728, 728], replicated
- grad_later: float32 [2, 256, 256], replicated
The draws below stay inside these ranges and needn't reach their ends.
Inputs may be any that keep to these rules, and one draw needn't show every extreme that they name: `rate_first`: at least one of the two rates equals 6. `rates_later`: at least one of the rates equals 21.
All inputs are finite; a program needn't handle non-finite values.
Results may differ from the reference program's by a relative error of at most 0.015.
Values may be sent and summed in bfloat16 or wider, within the bound.
A program may use at most 128 MiB of HBM per device.

```python
import jax
import jax.numpy as jnp
from jax import lax

C = 728
CH = 2048
B = 256
LATER = 2
R0 = 6
RMAX = 21
MB = 2
H = 96
W = 96


def draw_rate_first(key, part):
    values = jax.random.randint(key, (2,), 1, R0 + 1)
    chosen = jax.random.randint(jax.random.fold_in(key, 11), (), 0, 2)
    return jnp.where(jnp.arange(2) == chosen, R0, values).astype(jnp.int32)


def draw_rates_later(key, part):
    values = jax.random.randint(key, (LATER, 2), 1, RMAX + 1)
    chosen = jax.random.randint(jax.random.fold_in(key, 13), (), 0, LATER * 2)
    places = jnp.arange(LATER * 2).reshape(LATER, 2)
    return jnp.where(places == chosen, RMAX, values).astype(jnp.int32)


def levels(rng, dims, cuts, smallest, high):
    def one(dim, blocks):
        steps = jax.random.uniform(jax.random.fold_in(jax.random.fold_in(rng, 6), dim), (blocks,), jnp.float32, smallest / len(cuts), high / len(cuts))
        return jnp.repeat(jnp.exp(steps), dims[dim] // blocks).reshape((-1,) + (1,) * (len(dims) - dim - 1))

    factor_of = one(*cuts[0])
    for cut in cuts[1:]:
        factor_of = factor_of * one(*cut)
    return factor_of


def centred(key, extent, spread, bound, split=(), held_as=jnp.bfloat16):
    entries = spread * jax.random.normal(key, extent, jnp.float32)
    if split:
        entries = entries * levels(key, extent, split, -0.22, 0.18)
    return jnp.clip(entries, -bound, bound).astype(held_as)


def setup_inputs(seed: int = 0) -> dict:
    key_list = jax.random.split(jax.random.key(seed), 13)
    return {
        "features": centred(key_list[0], (MB, H, W, C), 1.0, 6.0, ((1, 16),)),
        "upstream": centred(key_list[1], (MB, H, W, B), ((MB * H * W) ** -0.5), 0.046875, ((1, 4), (2, 4))),
        "depth_mid": centred(key_list[2], (9, C), 9 ** -0.5, 2.0, (), jnp.float32),
        "point_mid": centred(key_list[3], (C, C), C ** -0.5, 0.21875),
        "projection": centred(key_list[4], (C, CH), C ** -0.5, 0.21875),
        "depth_first": centred(key_list[5], (9, CH), 9 ** -0.5, 2.0, (), jnp.float32),
        "point_first": centred(key_list[6], (CH, B), CH ** -0.5, 0.125),
        "depth_later": centred(key_list[7], (LATER, 9, B), 9 ** -0.5, 2.0, (), jnp.float32),
        "point_later": centred(key_list[8], (LATER, B, B), B ** -0.5, 0.375),
        "joining": centred(key_list[9], ((LATER + 1) * B, B), ((LATER + 1) * B) ** -0.5, 0.21875),
        "rate_first": draw_rate_first(jax.random.fold_in(key_list[12], 71), 0),
        "rates_later": draw_rates_later(jax.random.fold_in(key_list[12], 71), 0),
    }


def silu_slope(argument):
    sigmoid_value = jax.nn.sigmoid(argument)
    return sigmoid_value * (1.0 + argument * (1.0 - sigmoid_value))


def dilated(field, weights, rates_pair, margin, direction):
    padded = jnp.pad(field, ((margin, margin), (margin, margin), (0, 0)))
    height, breadth, depth = field.shape
    summed = jnp.zeros(field.shape, jnp.float32)
    for row_step in (-1, 0, 1):
        for col_step in (-1, 0, 1):
            row_start = (margin + direction * row_step * rates_pair[0]).astype(jnp.int32)
            col_start = (margin + direction * col_step * rates_pair[1]).astype(jnp.int32)
            window = lax.dynamic_slice(padded, (row_start, col_start, jnp.zeros((), jnp.int32)), (height, breadth, depth))
            summed = summed + window.astype(jnp.float32) * weights[3 * (row_step + 1) + col_step + 1]
    return summed


def matmul(left, right):
    flat = left.reshape(-1, left.shape[2])
    result = jnp.dot(flat, right, preferred_element_type=jnp.float32)
    return result.reshape(left.shape[0], left.shape[1], right.shape[1])


def gram(left, right):
    return jnp.dot(left.reshape(-1, left.shape[2]).T, right.reshape(-1, right.shape[2]), preferred_element_type=jnp.float32)


def reference(features, upstream, depth_mid, point_mid, projection, depth_first, point_first, depth_later, point_later, joining, rate_first, rates_later):
    unit_rates = jnp.ones((2,), jnp.int32)
    channels = point_later.shape[1]

    def micro_batch(operands):
        features_now, upstream_now = operands
        activated = jax.nn.silu(features_now.astype(jnp.float32))
        mid_conv = dilated(activated, depth_mid, unit_rates, 1, 1).astype(jnp.bfloat16)
        section_out = (features_now.astype(jnp.float32) + matmul(mid_conv, point_mid)).astype(jnp.bfloat16)
        projected = matmul(section_out, projection).astype(jnp.bfloat16)
        first_conv = dilated(projected, depth_first, rate_first, R0, 1).astype(jnp.bfloat16)
        first_pre = matmul(first_conv, point_first)
        first_out = jax.nn.silu(first_pre).astype(jnp.bfloat16)
        upstream_back = matmul(upstream_now, joining.T)
        first_back = upstream_back[:, :, :channels]
        branch_grads = []
        for branch in range(LATER):
            later_conv = dilated(first_out, depth_later[branch], rates_later[branch], RMAX, 1).astype(jnp.bfloat16)
            later_pre = matmul(later_conv, point_later[branch])
            block = upstream_back[:, :, (branch + 1) * channels:(branch + 2) * channels]
            later_gate = (block * silu_slope(later_pre)).astype(jnp.bfloat16)
            later_back = matmul(later_gate, point_later[branch].T).astype(jnp.bfloat16)
            branch_grads.append(gram(later_conv, later_gate))
            first_back = first_back + dilated(later_back, depth_later[branch], rates_later[branch], RMAX, -1)
        first_gate = (first_back * silu_slope(first_pre)).astype(jnp.bfloat16)
        conv_back = matmul(first_gate, point_first.T).astype(jnp.bfloat16)
        projected_back = dilated(conv_back, depth_first, rate_first, R0, -1).astype(jnp.bfloat16)
        section_back = matmul(projected_back, projection.T).astype(jnp.bfloat16)
        return gram(mid_conv, section_back), jnp.stack(branch_grads)

    mid_terms, later_terms = lax.map(micro_batch, (features, upstream))
    return jnp.sum(mid_terms, axis=0), jnp.sum(later_terms, axis=0)
```

```python
import jax
import jax.numpy as jnp
from jax import lax
from jax.sharding import PartitionSpec as P

LATER = 2
R0 = 6
RMAX = 21


def as_sent(value):
    return jax.tree.map(lambda a: a.astype(jnp.bfloat16) if a.dtype == jnp.float32 else a, value)


def with_halo(cells, sides, width):
    for axis, dim in sides:
        count = lax.axis_size(axis)
        ends = count - 1
        head = lax.slice_in_dim(cells, 0, width, axis=dim)
        tail = lax.slice_in_dim(cells, cells.shape[dim] - width, cells.shape[dim], axis=dim)
        cells = jnp.concatenate(
            [
                lax.ppermute(tail, axis, [(i, (i + 1) % count) for i in range(ends)]),
                cells,
                lax.ppermute(head, axis, [((i + 1) % count, i) for i in range(ends)]),
            ],
            axis=dim,
        )
    return cells


def silu_slope(argument):
    sigmoid_value = jax.nn.sigmoid(argument)
    return sigmoid_value * (1.0 + argument * (1.0 - sigmoid_value))


def dilated(padded, weights, rates_pair, margin, height, breadth, direction):
    depth = padded.shape[2]
    summed = jnp.zeros((height, breadth, depth), jnp.float32)
    for row_step in (-1, 0, 1):
        for col_step in (-1, 0, 1):
            row_start = margin + direction * row_step * rates_pair[0]
            col_start = margin + direction * col_step * rates_pair[1]
            window = lax.dynamic_slice(
                padded, (row_start, col_start, jnp.zeros((), jnp.int32)), (height, breadth, depth)
            )
            summed = (
                summed + window.astype(jnp.float32) * weights[3 * (row_step + 1) + col_step + 1]
            )
    return summed


def extend_tile(field, margin):
    return with_halo(as_sent(field), (("cols", 1), ("rows", 0)), margin).astype(field.dtype)


def backbone_local(haloed, features_now, depth_mid, point_mid):
    activated = jax.nn.silu(haloed.astype(jnp.float32))
    height, breadth, depth = features_now.shape
    mid_conv = jnp.zeros((height, breadth, depth), jnp.float32)
    for row in range(3):
        for col in range(3):
            mid_conv = (
                mid_conv
                + activated[row : row + height, col : col + breadth] * depth_mid[3 * row + col]
            )
    mid_conv = mid_conv.astype(jnp.bfloat16)
    mixed = jnp.einsum("hwc,cd->hwd", mid_conv, point_mid, preferred_element_type=jnp.float32)
    section_out = (features_now.astype(jnp.float32) + mixed).astype(jnp.bfloat16)
    return (section_out, mid_conv)


def mid_gradient(mid_conv, section_back):
    return jnp.einsum("hwc,hwd->cd", mid_conv, section_back, preferred_element_type=jnp.float32)


def project(field, projection):
    return jnp.einsum("hwc,ck->hwk", field, projection, preferred_element_type=jnp.float32).astype(
        jnp.bfloat16
    )


def head_front(padded_proj, depth_first, point_first, rate_first):
    height = padded_proj.shape[0] - 2 * R0
    breadth = padded_proj.shape[1] - 2 * R0
    first_conv = dilated(padded_proj, depth_first, rate_first, R0, height, breadth, 1).astype(
        jnp.bfloat16
    )
    first_pre = jnp.einsum(
        "hwc,cd->hwd", first_conv, point_first, preferred_element_type=jnp.float32
    )
    return (jax.nn.silu(first_pre).astype(jnp.bfloat16), first_pre)


def head_middle(padded_first, upstream_now, depth_later, point_later, rates_later, joining):
    height, breadth, channels = upstream_now.shape
    upstream_back = jnp.einsum(
        "hwb,kb->hwk", upstream_now, joining, preferred_element_type=jnp.float32
    )
    branch_backs = []
    branch_grads = []
    for branch in range(LATER):
        later_conv = dilated(
            padded_first, depth_later[branch], rates_later[branch], RMAX, height, breadth, 1
        ).astype(jnp.bfloat16)
        later_pre = jnp.einsum(
            "hwc,cd->hwd", later_conv, point_later[branch], preferred_element_type=jnp.float32
        )
        block = upstream_back[:, :, (branch + 1) * channels : (branch + 2) * channels]
        later_gate = (block * silu_slope(later_pre)).astype(jnp.bfloat16)
        later_back = jnp.einsum(
            "hwd,cd->hwc", later_gate, point_later[branch], preferred_element_type=jnp.float32
        )
        branch_backs.append(later_back.astype(jnp.bfloat16))
        branch_grads.append(
            jnp.einsum("hwc,hwd->cd", later_conv, later_gate, preferred_element_type=jnp.float32)
        )
    return (
        jnp.concatenate(branch_backs, axis=2),
        jnp.stack(branch_grads),
        upstream_back[:, :, :channels],
    )


def head_back(padded_backs, first_direct, first_pre, depth_later, rates_later):
    height, breadth, channels = first_direct.shape
    first_back = first_direct
    for branch in range(LATER):
        portion = padded_backs[:, :, branch * channels : (branch + 1) * channels]
        first_back = first_back + dilated(
            portion, depth_later[branch], rates_later[branch], RMAX, height, breadth, -1
        )
    return (first_back * silu_slope(first_pre)).astype(jnp.bfloat16)


def conv_gradient(padded_gate, point_first):
    return jnp.einsum(
        "hwd,cd->hwc", padded_gate, point_first, preferred_element_type=jnp.float32
    ).astype(jnp.bfloat16)


def head_end(padded_conv, depth_first, rate_first, projection):
    height = padded_conv.shape[0] - 2 * R0
    breadth = padded_conv.shape[1] - 2 * R0
    projected_back = dilated(padded_conv, depth_first, rate_first, R0, height, breadth, -1).astype(
        jnp.bfloat16
    )
    section_back = jnp.einsum(
        "hwk,ck->hwc", projected_back, projection, preferred_element_type=jnp.float32
    )
    return section_back.astype(jnp.bfloat16)


def local(
    features,
    upstream,
    depth_mid,
    point_mid,
    projection,
    depth_first,
    point_first,
    depth_later,
    point_later,
    joining,
    rate_first,
    rates_later,
):
    sections = lax.axis_size("section")
    section = lax.axis_index("section")
    micro_count = features.shape[0]
    channels_mid = features.shape[3]
    channels_head = point_later.shape[1]
    grad_mid = jnp.zeros((channels_mid, channels_mid), jnp.float32)
    grad_later = jnp.zeros((LATER, channels_head, channels_head), jnp.float32)
    for turn in range(micro_count // sections):
        micro = turn * sections + section
        slab = lax.dynamic_index_in_dim(features, micro, 0, keepdims=False)
        upstream_now = lax.dynamic_index_in_dim(upstream, micro, 0, keepdims=False)
        tile = lax.all_to_all(slab, "cols", split_axis=1, concat_axis=0, tiled=True)
        section_out, mid_conv = backbone_local(extend_tile(tile, 1), tile, depth_mid, point_mid)
        padded_proj = project(extend_tile(section_out, R0), projection)
        first_out, first_pre = head_front(padded_proj, depth_first, point_first, rate_first)
        branch_backs, later_terms, first_direct = head_middle(
            extend_tile(first_out, RMAX),
            upstream_now,
            depth_later,
            point_later,
            rates_later,
            joining,
        )
        first_gate = head_back(
            extend_tile(branch_backs, RMAX), first_direct, first_pre, depth_later, rates_later
        )
        padded_conv = conv_gradient(extend_tile(first_gate, R0), point_first)
        section_back = head_end(padded_conv, depth_first, rate_first, projection)
        grad_mid = grad_mid + mid_gradient(mid_conv, section_back)
        grad_later = grad_later + later_terms
    grad_later = lax.psum(grad_later, ("section", "rows", "cols"))
    grad_mid = lax.psum(grad_mid, ("section", "rows", "cols"))
    return (grad_mid, grad_later)


def solution(mesh):
    placed = (
        P(None, ("rows", "cols"), None, None),
        P(None, "rows", "cols", None),
        P(),
        P(),
        P(),
        P(),
        P(),
        P(),
        P(),
        P(),
        P(),
        P(),
    )
    return jax.shard_map(local, mesh=mesh, in_specs=placed, out_specs=(P(), P()), check_vma=False)
```

```python
import functools

import jax
import jax.numpy as jnp
from jax import lax
from jax.experimental import pallas as pl
from jax.experimental.pallas import tpu as pltpu
from jax.sharding import PartitionSpec as P

LATER = 2
R0 = 6
RMAX = 21


def as_sent(value):
    return jax.tree.map(lambda a: a.astype(jnp.bfloat16) if a.dtype == jnp.float32 else a, value)


def with_halo(cells, sides, width):
    for axis, dim in sides:
        count = lax.axis_size(axis)
        ends = count - 1
        head = lax.slice_in_dim(cells, 0, width, axis=dim)
        tail = lax.slice_in_dim(cells, cells.shape[dim] - width, cells.shape[dim], axis=dim)
        cells = jnp.concatenate(
            [
                lax.ppermute(tail, axis, [(i, (i + 1) % count) for i in range(ends)]),
                cells,
                lax.ppermute(head, axis, [((i + 1) % count, i) for i in range(ends)]),
            ],
            axis=dim,
        )
    return cells


def silu_slope(argument):
    sigmoid_value = jax.nn.sigmoid(argument)
    return sigmoid_value * (1.0 + argument * (1.0 - sigmoid_value))


def dilated(padded, weights, rates_pair, margin, height, breadth, direction):
    depth = padded.shape[2]
    summed = jnp.zeros((height, breadth, depth), jnp.float32)
    for row_step in (-1, 0, 1):
        for col_step in (-1, 0, 1):
            row_start = margin + direction * row_step * rates_pair[0]
            col_start = margin + direction * col_step * rates_pair[1]
            window = lax.dynamic_slice(
                padded, (row_start, col_start, jnp.zeros((), jnp.int32)), (height, breadth, depth)
            )
            summed = (
                summed + window.astype(jnp.float32) * weights[3 * (row_step + 1) + col_step + 1]
            )
    return summed


def extend_tile(field, margin):
    return with_halo(as_sent(field), (("cols", 1), ("rows", 0)), margin).astype(field.dtype)


def backbone_local(haloed, features_now, depth_mid, point_mid):
    activated = jax.nn.silu(haloed.astype(jnp.float32))
    height, breadth, depth = features_now.shape
    mid_conv = jnp.zeros((height, breadth, depth), jnp.float32)
    for row in range(3):
        for col in range(3):
            mid_conv = (
                mid_conv
                + activated[row : row + height, col : col + breadth] * depth_mid[3 * row + col]
            )
    mid_conv = mid_conv.astype(jnp.bfloat16)
    mixed = jnp.einsum("hwc,cd->hwd", mid_conv, point_mid, preferred_element_type=jnp.float32)
    section_out = (features_now.astype(jnp.float32) + mixed).astype(jnp.bfloat16)
    return (section_out, mid_conv)


def mid_gradient(mid_conv, section_back):
    return jnp.einsum("hwc,hwd->cd", mid_conv, section_back, preferred_element_type=jnp.float32)


def project(field, projection):
    return jnp.einsum("hwc,ck->hwk", field, projection, preferred_element_type=jnp.float32).astype(
        jnp.bfloat16
    )


def head_front(padded_proj, depth_first, point_first, rate_first):
    height = padded_proj.shape[0] - 2 * R0
    breadth = padded_proj.shape[1] - 2 * R0
    first_conv = dilated(padded_proj, depth_first, rate_first, R0, height, breadth, 1).astype(
        jnp.bfloat16
    )
    first_pre = jnp.einsum(
        "hwc,cd->hwd", first_conv, point_first, preferred_element_type=jnp.float32
    )
    return (jax.nn.silu(first_pre).astype(jnp.bfloat16), first_pre)


def head_middle(padded_first, upstream_now, depth_later, point_later, rates_later, joining):
    height, breadth, channels = upstream_now.shape
    upstream_back = jnp.einsum(
        "hwb,kb->hwk", upstream_now, joining, preferred_element_type=jnp.float32
    )
    branch_backs = []
    branch_grads = []
    for branch in range(LATER):
        later_conv = dilated(
            padded_first, depth_later[branch], rates_later[branch], RMAX, height, breadth, 1
        ).astype(jnp.bfloat16)
        later_pre = jnp.einsum(
            "hwc,cd->hwd", later_conv, point_later[branch], preferred_element_type=jnp.float32
        )
        block = upstream_back[:, :, (branch + 1) * channels : (branch + 2) * channels]
        later_gate = (block * silu_slope(later_pre)).astype(jnp.bfloat16)
        later_back = jnp.einsum(
            "hwd,cd->hwc", later_gate, point_later[branch], preferred_element_type=jnp.float32
        )
        branch_backs.append(later_back.astype(jnp.bfloat16))
        branch_grads.append(
            jnp.einsum("hwc,hwd->cd", later_conv, later_gate, preferred_element_type=jnp.float32)
        )
    return (
        jnp.concatenate(branch_backs, axis=2),
        jnp.stack(branch_grads),
        upstream_back[:, :, :channels],
    )


def head_back(padded_backs, first_direct, first_pre, depth_later, rates_later):
    height, breadth, channels = first_direct.shape
    first_back = first_direct
    for branch in range(LATER):
        portion = padded_backs[:, :, branch * channels : (branch + 1) * channels]
        first_back = first_back + dilated(
            portion, depth_later[branch], rates_later[branch], RMAX, height, breadth, -1
        )
    return (first_back * silu_slope(first_pre)).astype(jnp.bfloat16)


def conv_gradient(padded_gate, point_first):
    return jnp.einsum(
        "hwd,cd->hwc", padded_gate, point_first, preferred_element_type=jnp.float32
    ).astype(jnp.bfloat16)


def head_end(padded_conv, depth_first, rate_first, projection):
    height = padded_conv.shape[0] - 2 * R0
    breadth = padded_conv.shape[1] - 2 * R0
    projected_back = dilated(padded_conv, depth_first, rate_first, R0, height, breadth, -1).astype(
        jnp.bfloat16
    )
    section_back = jnp.einsum(
        "hwk,ck->hwc", projected_back, projection, preferred_element_type=jnp.float32
    )
    return section_back.astype(jnp.bfloat16)


LANES = 256
STREAMS = (("core", "section", "pair", "cols"), ("core", "pair", "section", "cols"))


def total_kernel(sizes, x_ref, out_ref, acc, gathered, *rest):
    steps = len(STREAMS[0])
    sends = rest[: 2 * steps]
    recvs = rest[2 * steps : 4 * steps]
    send_sem, recv_sem = rest[4 * steps :]
    row = lax.axis_index("rows")
    place = {
        "core": lax.rem(row, 2),
        "pair": lax.div(row, 2),
        "section": lax.axis_index("section"),
        "cols": lax.axis_index("cols"),
    }

    def peer(stage, hop):
        spot = dict(place)
        spot[stage] = lax.rem(place[stage] + hop, sizes[stage])
        return spot[stage], (spot["section"], spot["pair"] * 2 + spot["core"], spot["cols"])

    barrier = pltpu.get_barrier_semaphore()
    count = 0
    for stage in STREAMS[0]:
        for hop in range(1, sizes[stage]):
            pl.semaphore_signal(
                barrier, inc=1, device_id=peer(stage, hop)[1], device_id_type=pl.DeviceIdType.MESH
            )
            count += 1
    pl.semaphore_wait(barrier, count)

    half = x_ref.shape[0] // 2
    starts = [0, half]
    spans = [half, half]
    history = [[], []]
    for step in range(steps):
        flying = []
        source = x_ref if step == 0 else acc
        for stream in range(2):
            stage = STREAMS[stream][step]
            parts = sizes[stage]
            span = spans[stream] // parts
            slot = 2 * step + stream
            for hop in range(1, parts):
                index, target = peer(stage, hop)
                begin = pl.multiple_of(starts[stream] + index * span, 16)
                sends[slot][hop - 1] = source[pl.ds(begin, span), :].astype(jnp.bfloat16)
                copy = pltpu.make_async_remote_copy(
                    src_ref=sends[slot].at[hop - 1],
                    dst_ref=recvs[slot].at[hop - 1],
                    send_sem=send_sem.at[slot, hop - 1],
                    recv_sem=recv_sem.at[slot, hop - 1],
                    device_id=target,
                    device_id_type=pl.DeviceIdType.MESH,
                )
                copy.start()
                flying.append(copy)
        for copy in flying:
            copy.wait()
        for stream in range(2):
            stage = STREAMS[stream][step]
            parts = sizes[stage]
            spans[stream] = spans[stream] // parts
            starts[stream] = pl.multiple_of(
                starts[stream] + place[stage] * spans[stream], 16
            )
            slot = 2 * step + stream
            here = pl.ds(starts[stream], spans[stream])
            summed = source[here, :]
            for hop in range(1, parts):
                summed = summed + recvs[slot][hop - 1].astype(jnp.float32)
            acc[here, :] = summed
            history[stream].append((starts[stream], spans[stream]))
    for stream in range(2):
        here = pl.ds(starts[stream], spans[stream])
        gathered[here, :] = acc[here, :].astype(jnp.bfloat16)
    for step in reversed(range(steps)):
        flying = []
        for stream in range(2):
            stage = STREAMS[stream][step]
            begin, span = history[stream][step]
            slot = 2 * steps + 2 * step + stream
            for hop in range(1, sizes[stage]):
                block = gathered.at[pl.ds(begin, span), :]
                copy = pltpu.make_async_remote_copy(
                    src_ref=block,
                    dst_ref=block,
                    send_sem=send_sem.at[slot, hop - 1],
                    recv_sem=recv_sem.at[slot, hop - 1],
                    device_id=peer(stage, hop)[1],
                    device_id_type=pl.DeviceIdType.MESH,
                )
                copy.start()
                flying.append(copy)
        for copy in flying:
            copy.wait()
    out_ref[...] = gathered[...].astype(jnp.float32)


def total_over_devices(terms):
    rows_count = lax.axis_size("rows")
    sizes = {
        "core": 2,
        "pair": rows_count // 2,
        "section": lax.axis_size("section"),
        "cols": lax.axis_size("cols"),
    }
    length = terms.shape[0]
    sends = []
    for step in range(len(STREAMS[0])):
        for stream in range(2):
            span = length // 2
            for stage in STREAMS[stream][: step + 1]:
                span = span // sizes[stage]
            parts = sizes[STREAMS[stream][step]]
            sends.append(pltpu.VMEM((parts - 1, span, LANES), jnp.bfloat16))
    slots = 4 * len(STREAMS[0])
    most = max(sizes.values()) - 1
    return pl.pallas_call(
        functools.partial(total_kernel, sizes),
        out_shape=jax.ShapeDtypeStruct(terms.shape, jnp.float32),
        in_specs=[pl.BlockSpec(memory_space=pltpu.VMEM)],
        out_specs=pl.BlockSpec(memory_space=pltpu.VMEM),
        scratch_shapes=[
            pltpu.VMEM(terms.shape, jnp.float32),
            pltpu.VMEM(terms.shape, jnp.bfloat16),
            *sends,
            *sends,
            pltpu.SemaphoreType.DMA((slots, most)),
            pltpu.SemaphoreType.DMA((slots, most)),
        ],
        compiler_params=pltpu.CompilerParams(
            collective_id=0, has_side_effects=True, vmem_limit_bytes=40 * 1024 * 1024
        ),
    )(terms)


def total_gradients(grad_mid, grad_later):
    devices = lax.axis_size("section") * lax.axis_size("rows") * lax.axis_size("cols")
    channels = grad_mid.shape[0]
    columns = -(-channels // LANES)
    wide = jnp.pad(grad_mid, ((0, 0), (0, columns * LANES - channels)))
    pieces = [wide[:, i * LANES : (i + 1) * LANES] for i in range(columns)]
    pieces.append(grad_later.reshape(-1, LANES))
    used = sum(piece.shape[0] for piece in pieces)
    unit = 32 * devices
    length = -(-used // unit) * unit
    pieces.append(jnp.zeros((length - used, LANES), jnp.float32))
    summed = total_over_devices(jnp.concatenate(pieces, axis=0))
    wide = jnp.concatenate(
        [summed[i * channels : (i + 1) * channels] for i in range(columns)], axis=1
    )
    later = summed[columns * channels : used].reshape(grad_later.shape)
    return (wide[:, :channels], later)


def local(
    features,
    upstream,
    depth_mid,
    point_mid,
    projection,
    depth_first,
    point_first,
    depth_later,
    point_later,
    joining,
    rate_first,
    rates_later,
):
    sections = lax.axis_size("section")
    section = lax.axis_index("section")
    micro_count = features.shape[0]
    channels_mid = features.shape[3]
    channels_head = point_later.shape[1]
    grad_mid = jnp.zeros((channels_mid, channels_mid), jnp.float32)
    grad_later = jnp.zeros((LATER, channels_head, channels_head), jnp.float32)
    for turn in range(micro_count // sections):
        micro = turn * sections + section
        slab = lax.dynamic_index_in_dim(features, micro, 0, keepdims=False)
        upstream_now = lax.dynamic_index_in_dim(upstream, micro, 0, keepdims=False)
        tile = lax.all_to_all(slab, "cols", split_axis=1, concat_axis=0, tiled=True)
        section_out, mid_conv = backbone_local(extend_tile(tile, 1), tile, depth_mid, point_mid)
        padded_proj = project(extend_tile(section_out, R0), projection)
        first_out, first_pre = head_front(padded_proj, depth_first, point_first, rate_first)
        branch_backs, later_terms, first_direct = head_middle(
            extend_tile(first_out, RMAX),
            upstream_now,
            depth_later,
            point_later,
            rates_later,
            joining,
        )
        first_gate = head_back(
            extend_tile(branch_backs, RMAX), first_direct, first_pre, depth_later, rates_later
        )
        padded_conv = conv_gradient(extend_tile(first_gate, R0), point_first)
        section_back = head_end(padded_conv, depth_first, rate_first, projection)
        grad_mid = grad_mid + mid_gradient(mid_conv, section_back)
        grad_later = grad_later + later_terms
    return total_gradients(grad_mid, grad_later)


def solution(mesh):
    placed = (
        P(None, ("rows", "cols"), None, None),
        P(None, "rows", "cols", None),
        P(),
        P(),
        P(),
        P(),
        P(),
        P(),
        P(),
        P(),
        P(),
        P(),
    )
    return jax.shard_map(local, mesh=mesh, in_specs=placed, out_specs=(P(), P()), check_vma=False)
```

```python
import functools

import jax
import jax.numpy as jnp
from jax import lax
from jax.experimental import pallas as pl
from jax.experimental.pallas import tpu as pltpu
from jax.sharding import PartitionSpec as P

LATER = 2
R0 = 6
RMAX = 21


def as_sent(value):
    return jax.tree.map(lambda a: a.astype(jnp.bfloat16) if a.dtype == jnp.float32 else a, value)


def with_halo(cells, sides, width):
    for axis, dim in sides:
        count = lax.axis_size(axis)
        ends = count - 1
        head = lax.slice_in_dim(cells, 0, width, axis=dim)
        tail = lax.slice_in_dim(cells, cells.shape[dim] - width, cells.shape[dim], axis=dim)
        cells = jnp.concatenate(
            [
                lax.ppermute(tail, axis, [(i, (i + 1) % count) for i in range(ends)]),
                cells,
                lax.ppermute(head, axis, [((i + 1) % count, i) for i in range(ends)]),
            ],
            axis=dim,
        )
    return cells


def silu_slope(argument):
    sigmoid_value = jax.nn.sigmoid(argument)
    return sigmoid_value * (1.0 + argument * (1.0 - sigmoid_value))


def dilated(padded, weights, rates_pair, margin, height, breadth, direction):
    depth = padded.shape[2]
    summed = jnp.zeros((height, breadth, depth), jnp.float32)
    for row_step in (-1, 0, 1):
        for col_step in (-1, 0, 1):
            row_start = margin + direction * row_step * rates_pair[0]
            col_start = margin + direction * col_step * rates_pair[1]
            window = lax.dynamic_slice(
                padded, (row_start, col_start, jnp.zeros((), jnp.int32)), (height, breadth, depth)
            )
            summed = (
                summed + window.astype(jnp.float32) * weights[3 * (row_step + 1) + col_step + 1]
            )
    return summed


def extend_tile(field, margin):
    return with_halo(as_sent(field), (("cols", 1), ("rows", 0)), margin).astype(field.dtype)


def backbone_local(haloed, features_now, depth_mid, point_mid):
    activated = jax.nn.silu(haloed.astype(jnp.float32))
    height, breadth, depth = features_now.shape
    mid_conv = jnp.zeros((height, breadth, depth), jnp.float32)
    for row in range(3):
        for col in range(3):
            mid_conv = (
                mid_conv
                + activated[row : row + height, col : col + breadth] * depth_mid[3 * row + col]
            )
    mid_conv = mid_conv.astype(jnp.bfloat16)
    mixed = jnp.einsum("hwc,cd->hwd", mid_conv, point_mid, preferred_element_type=jnp.float32)
    section_out = (features_now.astype(jnp.float32) + mixed).astype(jnp.bfloat16)
    return (section_out, mid_conv)


def mid_gradient(mid_conv, section_back):
    return jnp.einsum("hwc,hwd->cd", mid_conv, section_back, preferred_element_type=jnp.float32)


def project(field, projection):
    return jnp.einsum("hwc,ck->hwk", field, projection, preferred_element_type=jnp.float32).astype(
        jnp.bfloat16
    )


def head_front(padded_proj, depth_first, point_first, rate_first):
    height = padded_proj.shape[0] - 2 * R0
    breadth = padded_proj.shape[1] - 2 * R0
    first_conv = dilated(padded_proj, depth_first, rate_first, R0, height, breadth, 1).astype(
        jnp.bfloat16
    )
    first_pre = jnp.einsum(
        "hwc,cd->hwd", first_conv, point_first, preferred_element_type=jnp.float32
    )
    return (jax.nn.silu(first_pre).astype(jnp.bfloat16), first_pre)


def head_middle(padded_first, upstream_now, depth_later, point_later, rates_later, joining):
    height, breadth, channels = upstream_now.shape
    upstream_back = jnp.einsum(
        "hwb,kb->hwk", upstream_now, joining, preferred_element_type=jnp.float32
    )
    branch_backs = []
    branch_grads = []
    for branch in range(LATER):
        later_conv = dilated(
            padded_first, depth_later[branch], rates_later[branch], RMAX, height, breadth, 1
        ).astype(jnp.bfloat16)
        later_pre = jnp.einsum(
            "hwc,cd->hwd", later_conv, point_later[branch], preferred_element_type=jnp.float32
        )
        block = upstream_back[:, :, (branch + 1) * channels : (branch + 2) * channels]
        later_gate = (block * silu_slope(later_pre)).astype(jnp.bfloat16)
        later_back = jnp.einsum(
            "hwd,cd->hwc", later_gate, point_later[branch], preferred_element_type=jnp.float32
        )
        branch_backs.append(later_back.astype(jnp.bfloat16))
        branch_grads.append(
            jnp.einsum("hwc,hwd->cd", later_conv, later_gate, preferred_element_type=jnp.float32)
        )
    return (
        jnp.concatenate(branch_backs, axis=2),
        jnp.stack(branch_grads),
        upstream_back[:, :, :channels],
    )


def head_back(padded_backs, first_direct, first_pre, depth_later, rates_later):
    height, breadth, channels = first_direct.shape
    first_back = first_direct
    for branch in range(LATER):
        portion = padded_backs[:, :, branch * channels : (branch + 1) * channels]
        first_back = first_back + dilated(
            portion, depth_later[branch], rates_later[branch], RMAX, height, breadth, -1
        )
    return (first_back * silu_slope(first_pre)).astype(jnp.bfloat16)


def conv_gradient(padded_gate, point_first):
    return jnp.einsum(
        "hwd,cd->hwc", padded_gate, point_first, preferred_element_type=jnp.float32
    ).astype(jnp.bfloat16)


def head_end(padded_conv, depth_first, rate_first, projection):
    height = padded_conv.shape[0] - 2 * R0
    breadth = padded_conv.shape[1] - 2 * R0
    projected_back = dilated(padded_conv, depth_first, rate_first, R0, height, breadth, -1).astype(
        jnp.bfloat16
    )
    projected_back = lax.optimization_barrier(projected_back)
    section_back = jnp.einsum(
        "hwk,ck->hwc", projected_back, projection, preferred_element_type=jnp.float32
    )
    return section_back.astype(jnp.bfloat16)


LANES = 256
STREAMS = (("core", "section", "pair", "cols"), ("core", "pair", "section", "cols"))


def total_kernel(sizes, x_ref, out_ref, acc, gathered, *rest):
    steps = len(STREAMS[0])
    sends = rest[: 2 * steps]
    recvs = rest[2 * steps : 4 * steps]
    send_sem, recv_sem = rest[4 * steps :]
    row = lax.axis_index("rows")
    place = {
        "core": lax.rem(row, 2),
        "pair": lax.div(row, 2),
        "section": lax.axis_index("section"),
        "cols": lax.axis_index("cols"),
    }

    def peer(stage, hop):
        spot = dict(place)
        spot[stage] = lax.rem(place[stage] + hop, sizes[stage])
        return spot[stage], (spot["section"], spot["pair"] * 2 + spot["core"], spot["cols"])

    barrier = pltpu.get_barrier_semaphore()
    count = 0
    for stage in STREAMS[0]:
        for hop in range(1, sizes[stage]):
            pl.semaphore_signal(
                barrier, inc=1, device_id=peer(stage, hop)[1], device_id_type=pl.DeviceIdType.MESH
            )
            count += 1
    pl.semaphore_wait(barrier, count)

    half = x_ref.shape[0] // 2
    starts = [0, half]
    spans = [half, half]
    history = [[], []]
    for step in range(steps):
        flying = []
        source = x_ref if step == 0 else acc
        for stream in range(2):
            stage = STREAMS[stream][step]
            parts = sizes[stage]
            span = spans[stream] // parts
            slot = 2 * step + stream
            for hop in range(1, parts):
                index, target = peer(stage, hop)
                begin = pl.multiple_of(starts[stream] + index * span, 16)
                sends[slot][hop - 1] = source[pl.ds(begin, span), :].astype(jnp.bfloat16)
                copy = pltpu.make_async_remote_copy(
                    src_ref=sends[slot].at[hop - 1],
                    dst_ref=recvs[slot].at[hop - 1],
                    send_sem=send_sem.at[slot, hop - 1],
                    recv_sem=recv_sem.at[slot, hop - 1],
                    device_id=target,
                    device_id_type=pl.DeviceIdType.MESH,
                )
                copy.start()
                flying.append(copy)
        for copy in flying:
            copy.wait()
        for stream in range(2):
            stage = STREAMS[stream][step]
            parts = sizes[stage]
            spans[stream] = spans[stream] // parts
            starts[stream] = pl.multiple_of(
                starts[stream] + place[stage] * spans[stream], 16
            )
            slot = 2 * step + stream
            here = pl.ds(starts[stream], spans[stream])
            summed = source[here, :]
            for hop in range(1, parts):
                summed = summed + recvs[slot][hop - 1].astype(jnp.float32)
            acc[here, :] = summed
            history[stream].append((starts[stream], spans[stream]))
    for stream in range(2):
        here = pl.ds(starts[stream], spans[stream])
        gathered[here, :] = acc[here, :].astype(jnp.bfloat16)
    for step in reversed(range(steps)):
        flying = []
        for stream in range(2):
            stage = STREAMS[stream][step]
            begin, span = history[stream][step]
            slot = 2 * steps + 2 * step + stream
            for hop in range(1, sizes[stage]):
                block = gathered.at[pl.ds(begin, span), :]
                copy = pltpu.make_async_remote_copy(
                    src_ref=block,
                    dst_ref=block,
                    send_sem=send_sem.at[slot, hop - 1],
                    recv_sem=recv_sem.at[slot, hop - 1],
                    device_id=peer(stage, hop)[1],
                    device_id_type=pl.DeviceIdType.MESH,
                )
                copy.start()
                flying.append(copy)
        for copy in flying:
            copy.wait()
    out_ref[...] = gathered[...].astype(jnp.float32)


def total_over_devices(terms):
    rows_count = lax.axis_size("rows")
    sizes = {
        "core": 2,
        "pair": rows_count // 2,
        "section": lax.axis_size("section"),
        "cols": lax.axis_size("cols"),
    }
    length = terms.shape[0]
    sends = []
    for step in range(len(STREAMS[0])):
        for stream in range(2):
            span = length // 2
            for stage in STREAMS[stream][: step + 1]:
                span = span // sizes[stage]
            parts = sizes[STREAMS[stream][step]]
            sends.append(pltpu.VMEM((parts - 1, span, LANES), jnp.bfloat16))
    slots = 4 * len(STREAMS[0])
    most = max(sizes.values()) - 1
    return pl.pallas_call(
        functools.partial(total_kernel, sizes),
        out_shape=jax.ShapeDtypeStruct(terms.shape, jnp.float32),
        in_specs=[pl.BlockSpec(memory_space=pltpu.VMEM)],
        out_specs=pl.BlockSpec(memory_space=pltpu.VMEM),
        scratch_shapes=[
            pltpu.VMEM(terms.shape, jnp.float32),
            pltpu.VMEM(terms.shape, jnp.bfloat16),
            *sends,
            *sends,
            pltpu.SemaphoreType.DMA((slots, most)),
            pltpu.SemaphoreType.DMA((slots, most)),
        ],
        compiler_params=pltpu.CompilerParams(
            collective_id=0, has_side_effects=True, vmem_limit_bytes=40 * 1024 * 1024
        ),
    )(terms)


def total_gradients(grad_mid, grad_later):
    devices = lax.axis_size("section") * lax.axis_size("rows") * lax.axis_size("cols")
    channels = grad_mid.shape[0]
    columns = -(-channels // LANES)
    wide = jnp.pad(grad_mid, ((0, 0), (0, columns * LANES - channels)))
    pieces = [wide[:, i * LANES : (i + 1) * LANES] for i in range(columns)]
    pieces.append(grad_later.reshape(-1, LANES))
    used = sum(piece.shape[0] for piece in pieces)
    unit = 32 * devices
    length = -(-used // unit) * unit
    pieces.append(jnp.zeros((length - used, LANES), jnp.float32))
    summed = total_over_devices(jnp.concatenate(pieces, axis=0))
    wide = jnp.concatenate(
        [summed[i * channels : (i + 1) * channels] for i in range(columns)], axis=1
    )
    later = summed[columns * channels : used].reshape(grad_later.shape)
    return (wide[:, :channels], later)


def local(
    features,
    upstream,
    depth_mid,
    point_mid,
    projection,
    depth_first,
    point_first,
    depth_later,
    point_later,
    joining,
    rate_first,
    rates_later,
):
    sections = lax.axis_size("section")
    section = lax.axis_index("section")
    micro_count = features.shape[0]
    channels_mid = features.shape[3]
    channels_head = point_later.shape[1]
    grad_mid = jnp.zeros((channels_mid, channels_mid), jnp.float32)
    grad_later = jnp.zeros((LATER, channels_head, channels_head), jnp.float32)
    for turn in range(micro_count // sections):
        micro = turn * sections + section
        slab = lax.dynamic_index_in_dim(features, micro, 0, keepdims=False)
        upstream_now = lax.dynamic_index_in_dim(upstream, micro, 0, keepdims=False)
        groups = lax.axis_size("cols")
        breadth = slab.shape[1] // groups
        edged = jnp.pad(slab, ((0, 0), (1, 1), (0, 0)))
        blocks = jnp.concatenate(
            [edged[:, i * breadth : i * breadth + breadth + 2] for i in range(groups)], axis=0
        )
        wide = lax.all_to_all(blocks, "cols", split_axis=0, concat_axis=0, tiled=True)
        section_out, mid_conv = backbone_local(
            with_halo(wide, (("rows", 0),), 1), wide[:, 1:-1], depth_mid, point_mid
        )
        padded_proj = project(extend_tile(section_out, R0), projection)
        first_out, first_pre = head_front(padded_proj, depth_first, point_first, rate_first)
        branch_backs, later_terms, first_direct = head_middle(
            extend_tile(first_out, RMAX),
            upstream_now,
            depth_later,
            point_later,
            rates_later,
            joining,
        )
        first_gate = head_back(
            extend_tile(branch_backs, RMAX), first_direct, first_pre, depth_later, rates_later
        )
        padded_conv = conv_gradient(extend_tile(first_gate, R0), point_first)
        section_back = head_end(padded_conv, depth_first, rate_first, projection)
        section_back = lax.optimization_barrier(section_back)
        grad_mid = grad_mid + mid_gradient(mid_conv, section_back)
        grad_later = grad_later + later_terms
    return total_gradients(grad_mid, grad_later)


def solution(mesh):
    placed = (
        P(None, ("rows", "cols"), None, None),
        P(None, "rows", "cols", None),
        P(),
        P(),
        P(),
        P(),
        P(),
        P(),
        P(),
        P(),
        P(),
        P(),
    )
    return jax.shard_map(local, mesh=mesh, in_specs=placed, out_specs=(P(), P()), check_vma=False)
```
